128 devices in a mesh: frame: 16 (over y, x_hi, core), head: 8 (over x_lo, z).
Axes of the slice: x: 4 (x_hi: 2, x_lo: 2; x = x_hi * 2 + x_lo), y: 4, z: 4, core: 2. Of those that a mesh axis runs over, the one named last changes fastest.
Arguments:
- latents: bfloat16 [32, 1536, 1152], P('frame', 'head'), may hold values from -6 to 6
- modulation: float32 [6, 1152], replicated, may hold values from -3 to 3
- spatial_qkv: bfloat16 [1152, 3456], replicated, may hold values from -1 to 1
- spatial_out: bfloat16 [1152, 1152], replicated, may hold values from -0.1875 to 0.1875
- temporal_qkv: bfloat16 [1152, 3456], replicated, may hold values from -1 to 1
- temporal_out: bfloat16 [1152, 1152], replicated, may hold values from -0.1875 to 0.1875
Outputs:
- block_out: bfloat16 [32, 1536, 1152], P('frame', 'head')
The draws below stay inside these ranges and needn't reach their ends.
All inputs are finite; a program needn't handle non-finite values.
Results may differ from the reference program's by a relative error of at most 0.015.
Values may be sent and summed in bfloat16 or wider, within the bound.
A program may use at most 192 MiB of HBM per device.

```python
import math
import jax
import jax.numpy as jnp
from jax import lax

D = 1152
H = 16
HD = 72
F = 32
P_SIZE = 1536
N_HEAD = 8


def drawn_columns(key, strength):
    baseline_key, common_key, amplitude_key = jax.random.split(key, 3)
    baseline = jax.random.normal(baseline_key, (D, 3 * D), jnp.float32) * D ** (-0.5)
    common = jax.random.normal(common_key, (D, H, HD), jnp.float32) * D ** (-0.5)
    amplitude = jax.random.uniform(amplitude_key, (H,), jnp.float32, 0.0, strength)
    aligned = (common * jnp.sqrt(amplitude)[None, :, None]).reshape(D, D)
    combined = baseline + jnp.concatenate([aligned, aligned, jnp.zeros((D, D), jnp.float32)], 1)
    return jnp.clip(combined, -1.0, 1.0)


def draw_spatial_qkv(key, part):
    key = jax.random.fold_in(key, 7)
    return drawn_columns(key, 0.0).astype(jnp.bfloat16)


def draw_temporal_qkv(key, part):
    key = jax.random.fold_in(key, 13)
    return drawn_columns(key, 0.0).astype(jnp.bfloat16)


def steps_of(own_key, extent, shards, smallest, largest):
    def one(dim, blocks):
        draws = jax.random.uniform(jax.random.fold_in(jax.random.fold_in(own_key, 6), dim), (blocks,), jnp.float32, smallest / len(shards), largest / len(shards))
        return jnp.repeat(jnp.exp(draws), extent[dim] // blocks).reshape((-1,) + (1,) * (len(extent) - dim - 1))

    level = one(*shards[0])
    for cut in shards[1:]:
        level = level * one(*cut)
    return level


def noise(own_key, shape, scale, most, cuts=(), kind=jnp.bfloat16):
    values = jax.random.normal(own_key, shape, jnp.float32) * scale
    if len(cuts) > 0:
        values = steps_of(own_key, shape, cuts, -0.22, 0.18) * values
    return jnp.clip(values, min=-most, max=most).astype(kind)


def setup_inputs(seed: int = 0) -> dict:
    seeds = jax.random.split(jax.random.key(seed), 7)
    latents = noise(seeds[0], (F, P_SIZE, D), 1.0, 6.0, ((0, 16), (1, 8)))
    modulation = noise(seeds[1], (6, D), 0.5, 3.0, (), jnp.float32)
    spatial_qkv = draw_spatial_qkv(jax.random.fold_in(seeds[6], 71), 0)
    spatial_out = noise(seeds[3], (D, D), D ** -0.5, 0.1875)
    temporal_qkv = draw_temporal_qkv(jax.random.fold_in(seeds[6], 71), 0)
    temporal_out = noise(seeds[5], (D, D), D ** -0.5, 0.1875)
    return {"latents": latents, "modulation": modulation, "spatial_qkv": spatial_qkv, "spatial_out": spatial_out, "temporal_qkv": temporal_qkv, "temporal_out": temporal_out}


def normalize(tokens, offset, stretch):
    values = tokens.astype(jnp.float32)
    average = lax.optimization_barrier(jnp.mean(values, axis=-1, keepdims=True))
    centered = values - average
    variance = lax.optimization_barrier(jnp.mean(centered * centered, axis=-1, keepdims=True))
    normed = centered * lax.rsqrt(variance + 1e-06)
    return (normed * (1.0 + offset * 0.0 + stretch) + offset).astype(jnp.bfloat16)

def rotate(tensor, frames):
    half = tensor.shape[-1] // 2
    inverse = 10000.0 ** (-jnp.arange(half, dtype=jnp.float32) / half)
    angles = jnp.arange(frames, dtype=jnp.float32)[:, None] * inverse[None, :]
    angle_cos = jnp.cos(angles)[:, None, None, :]
    angle_sin = jnp.sin(angles)[:, None, None, :]
    leading = tensor[..., :half].astype(jnp.float32)
    trailing = tensor[..., half:].astype(jnp.float32)
    turned = jnp.concatenate([leading * angle_cos - trailing * angle_sin, leading * angle_sin + trailing * angle_cos], -1)
    return turned.astype(jnp.bfloat16)

def attend(queries, keys, values):
    scores = jnp.einsum('qbhe,kbhe->bhqk', queries.astype(jnp.float32), keys.astype(jnp.float32)) / math.sqrt(HD)
    weights_bf = jax.nn.softmax(scores, axis=-1).astype(jnp.bfloat16)
    mixed = jnp.einsum('bhqk,kbhe->qbhe', weights_bf.astype(jnp.float32), values.astype(jnp.float32))
    return mixed.astype(jnp.bfloat16)

def reference(latents, modulation, spatial_qkv, spatial_out, temporal_qkv, temporal_out):

    def spatial_frame(frame_tokens):
        normed = normalize(frame_tokens, modulation[0], modulation[1])
        projected = jnp.dot(normed, spatial_qkv, preferred_element_type=jnp.float32).astype(jnp.bfloat16)
        pieces = projected.reshape(P_SIZE, 1, 3, H, HD)
        outputs = attend(pieces[:, :, 0], pieces[:, :, 1], pieces[:, :, 2]).reshape(P_SIZE, D)
        projection = jnp.dot(outputs, spatial_out, preferred_element_type=jnp.float32)
        return (frame_tokens.astype(jnp.float32) + modulation[2] * projection).astype(jnp.bfloat16)
    middle = lax.map(spatial_frame, latents)
    groups = N_HEAD
    portion = P_SIZE // groups
    blocks = middle.reshape(F, groups, portion, D).transpose(1, 0, 2, 3)

    def temporal_block(tokens):
        normed = normalize(tokens, modulation[3], modulation[4])
        projected = jnp.dot(normed.reshape(F * portion, D), temporal_qkv, preferred_element_type=jnp.float32).astype(jnp.bfloat16)
        pieces = projected.reshape(F, portion, 3, H, HD)
        queries = rotate(pieces[:, :, 0], F)
        keys_rot = rotate(pieces[:, :, 1], F)
        outputs = attend(queries, keys_rot, pieces[:, :, 2]).reshape(F * portion, D)
        projection = jnp.dot(outputs, temporal_out, preferred_element_type=jnp.float32).reshape(F, portion, D)
        return (tokens.astype(jnp.float32) + modulation[5] * projection).astype(jnp.bfloat16)
    finished = lax.map(temporal_block, blocks)
    return finished.transpose(1, 0, 2, 3).reshape(F, P_SIZE, D)
```

```python
import math

import jax
import jax.numpy as jnp
import numpy as np
from jax import lax
from jax.experimental import pallas as pl
from jax.experimental.pallas import tpu as pltpu
from jax.sharding import PartitionSpec as P

MESH = pl.DeviceIdType.MESH
BF = jnp.bfloat16
F32 = jnp.float32
D, H, HD, F = 1152, 16, 72, 32
NH, NF = 8, 16
PAIR = 2 * HD
PATCH = 192
TOK = 2 * PATCH
KEYS = NH * PATCH
WIN = 5 * 128
SCALE = math.log2(math.e) / math.sqrt(HD)
NN = (((1,), (0,)), ((), ()))
NT = (((1,), (1,)), ((), ()))


def dot(a, b, dims=NN):
    return lax.dot_general(a, b, dims, preferred_element_type=F32)


def rope_table():
    inverse = 10000.0 ** (-np.arange(HD // 2) / (HD // 2))
    angles = np.arange(F)[:, None] * inverse[None, :]
    zeros = np.zeros_like(angles)
    cos = np.tile(np.concatenate([np.cos(angles)] * 2, 1), (1, H))
    low = np.tile(np.concatenate([-np.sin(angles), zeros], 1), (1, H))
    high = np.tile(np.concatenate([zeros, np.sin(angles)], 1), (1, H))
    rows = [t.reshape(NF, 2, D) for t in (cos, low, high, np.zeros((F, D)))]
    return np.concatenate(rows, 1).astype(np.float32)


def norm(x, offset, stretch):
    centered = x - jnp.mean(x, axis=-1, keepdims=True)
    variance = jnp.mean(centered * centered, axis=-1, keepdims=True)
    return centered * lax.rsqrt(variance + 1e-06) * (1.0 + stretch) + offset


def kernel(
    lat_h, mod, tab_h, wsq_h, wso_h, wtq_h, wto_h, out,
    lat, tab, wsq, wso, wtq, wto, load_sem,
    nrm, proj, recv, ks, vs, qs, sc, ob, ot, orecv, oa, mid, tin,
    ts, tsh, tr, trh, acc, acch, to, toh, ro, roh, bias,
    s_send, s_recv, r_send, r_recv, t_send, t_recv, th_send, th_recv,
    u_send, u_recv, uh_send, uh_recv,
):
    fi, hi = lax.axis_index("frame"), lax.axis_index("head")

    def at_head(k):
        return lax.rem(hi + k, NH)

    def at_frame(k):
        return lax.rem(fi + k, NF)

    def load(src, dst, i):
        return pltpu.make_async_copy(src, dst, load_sem.at[i])

    part_loads = [
        load(wsq_h.at[:, pl.ds(p * D, D)], wsq.at[:, pl.ds(p * D, D)], 2 + p) for p in range(3)
    ]
    loads = [
        load(lat_h, lat, 0), load(tab_h.at[fi], tab, 1), *part_loads,
        load(wso_h, wso, 5), load(wtq_h, wtq, 6), load(wto_h, wto, 7),
    ]
    for i in (0, 3, 4, 2, 1, 5, 6, 7):
        loads[i].start()

    barrier = pltpu.get_barrier_semaphore()

    def greet(k, _):
        pl.semaphore_signal(barrier, inc=1, device_id=(fi, at_head(k)), device_id_type=MESH)
        return 0

    def greet_frame(k, _):
        pl.semaphore_signal(barrier, inc=1, device_id=(at_frame(k), hi), device_id_type=MESH)
        return 0

    lax.fori_loop(1, NH, greet, 0)
    lax.fori_loop(1, NF, greet_frame, 0)

    def remote(src, dst, send, receive, device):
        return pltpu.make_async_remote_copy(
            src_ref=src, dst_ref=dst, send_sem=send, recv_sem=receive,
            device_id=device, device_id_type=MESH,
        )

    def await_bytes(ref, sem):
        pltpu.make_async_copy(ref, ref, sem).wait()

    loads[0].wait()
    for row, f, p, n in ((0, 0, 0, 128), (128, 1, 0, 128), (256, 0, 128, 64), (320, 1, 128, 64)):
        x = lat[f, p : p + n].astype(F32)
        nrm[row : row + n] = norm(x, mod[0:1], mod[1:2]).astype(BF)

    def piece(kind, ref, block):
        if kind < 2:
            return ref.at[kind, block]
        return ref.at[2, block, :, pl.ds(0, 256) if kind == 2 else pl.ds(256, 128)]

    def spatial_send(kinds):
        for kind in kinds:
            pltpu.make_async_copy(
                piece(kind, proj, hi), piece(kind, recv, hi), s_recv.at[kind, hi]
            ).start()

            def send(k, _):
                peer = at_head(k)
                remote(
                    piece(kind, proj, peer), piece(kind, recv, hi),
                    s_send.at[kind, peer], s_recv.at[kind, hi], (fi, peer),
                ).start()
                return 0

            lax.fori_loop(1, NH, send, 0)

    for slot, part in enumerate((1, 2, 0)):
        part_loads[part].wait()
        r = dot(nrm[...], wsq[:, part * D : (part + 1) * D])
        proj[slot] = r.astype(BF).T.reshape(NH, PAIR, TOK)
        if slot == 0:
            pl.semaphore_wait(barrier, NH + NF - 2)
        spatial_send(((0,), (1,), (2, 3))[slot])

    row = lax.broadcasted_iota(jnp.int32, (256, 256), 0) % 8
    col = lax.broadcasted_iota(jnp.int32, (256, 256), 1) % 8
    bias[...] = jnp.where(row == col, 0.0, -jnp.inf).astype(F32)

    vs[:, PAIR:, :] = jnp.ones((2, 16, KEYS), BF)
    lane = lax.broadcasted_iota(jnp.int32, (PAIR, 128), 1)

    def gather(kind, ref):
        def body(j, _):
            halves = []
            for b in range(2):
                src = 2 * j + b
                await_bytes(recv.at[kind, src], s_recv.at[kind, src])
                for f in range(2):
                    at = pl.multiple_of(src * 128, 128)
                    ref[f, 0:PAIR, pl.ds(at, 128)] = recv[kind, src, :, f * 128 : f * 128 + 128]
                halves.append(recv[kind, src, :, 256:384].astype(F32))
            a, b = halves
            at = pl.multiple_of(1024 + j * 128, 128)
            first = jnp.where(lane < 64, a, pltpu.roll(b, 64, 1))
            second = jnp.where(lane < 64, pltpu.roll(a, 64, 1), b)
            ref[0, 0:PAIR, pl.ds(at, 128)] = first.astype(BF)
            ref[1, 0:PAIR, pl.ds(at, 128)] = second.astype(BF)
            return 0

        lax.fori_loop(0, NH // 2, body, 0)

    gather(0, ks)
    gather(1, vs)

    def pair_source(i, b):
        return 2 * lax.rem(hi // 2 + i, 4) + b

    def quad_source(i, b):
        return 4 * lax.rem(hi // 4 + i - 4, 2) + b

    def take_pair(i):
        for b in range(2):
            src = pair_source(i, b)
            await_bytes(piece(2, recv, src), s_recv.at[2, src])
            for f in range(2):
                qs[i, f, b * 128 : b * 128 + 128] = recv[2, src, :, f * 128 : f * 128 + 128].T

    def take_quad(i):
        for b in range(4):
            src = quad_source(i, b)
            await_bytes(piece(3, recv, src), s_recv.at[3, src])
            q = recv[2, src, :, 256:384].T
            for f in range(2):
                qs[i, f, b * 64 : b * 64 + 64] = q[f * 64 : f * 64 + 64]

    column = lax.broadcasted_iota(jnp.int32, (256, PAIR), 1)

    def scores(i, f, h):
        q = qs[i, f]
        own = (column < HD) if h == 0 else (column >= HD)
        return dot(jnp.where(own, q, jnp.zeros_like(q)), ks[f])

    def mixed(s, f):
        p = jnp.exp2((s - jnp.max(s, axis=1, keepdims=True)) * SCALE).astype(BF)
        o = dot(p, vs[f], NT)
        return o[:, 0:PAIR] * (1.0 / o[:, PAIR : PAIR + 1])

    def give(kind, src):
        lanes = pl.ds(0, 256) if kind == 0 else pl.ds(256, 128)
        here, there = ot.at[src, :, lanes], orecv.at[hi, :, lanes]

        @pl.when(src == hi)
        def _():
            pltpu.make_async_copy(here, there, r_recv.at[kind, hi]).start()

        @pl.when(src != hi)
        def _():
            remote(here, there, r_send.at[kind, src], r_recv.at[kind, hi], (fi, src)).start()

    take_pair(0)
    sc[0] = scores(0, 0, 0)

    def attend(i, _):
        first = None
        for u in range(4):
            f, h = u // 2, u % 2
            if u == 3:

                @pl.when(i < 3)
                def _():
                    take_pair(i + 1)

                @pl.when((i >= 3) & (i < 5))
                def _():
                    take_quad(i + 1)

            later = jnp.minimum(i + 1, 5) if u == 3 else i
            s = sc[u % 2]
            sc[(u + 1) % 2] = scores(later, (u + 1) % 4 // 2, (u + 1) % 2)
            o = mixed(s, f)
            if h == 0:
                first = o
            else:
                ob[f] = jnp.where(column < HD, first, o).astype(BF)

        @pl.when(i < 4)
        def _():
            for f in range(2):
                o = ob[f].T
                for b in range(2):
                    ot[pair_source(i, b), :, f * 128 : f * 128 + 128] = o[:, b * 128 : b * 128 + 128]
            for b in range(2):
                give(0, pair_source(i, b))

        @pl.when(i >= 4)
        def _():
            for b in range(4):
                rows = pl.ds(b * 64, 64)
                o = jnp.concatenate([ob[0, rows], ob[1, rows]], 0)
                ot[quad_source(i, b), :, 256:384] = o.T
            for b in range(4):
                give(1, quad_source(i, b))

        return 0

    lax.fori_loop(0, 6, attend, 0)

    for i in (1, 5, 6):
        loads[i].wait()

    def finish_spatial(kind):
        def arrive(src, _):
            lanes = pl.ds(0, 256) if kind == 0 else pl.ds(256, 128)
            await_bytes(orecv.at[src, :, lanes], r_recv.at[kind, src])
            return 0

        lax.fori_loop(0, NH, arrive, 0)
        start, count = ((0, 256), (256, 128))[kind]
        for t in range(count // 128):
            at = start + t * 128
            oa[at : at + 128] = orecv[:, :, at : at + 128].reshape(D, 128).T
        r = dot(oa[start : start + count], wso[...])
        half = count // 2
        first = 128 * kind
        fresh = []
        for f in range(2):
            x = lat[f, first : first + half].astype(F32)
            m = (x + mod[2:3] * r[f * half : (f + 1) * half]).astype(BF)
            mid[f, first : first + half] = m
            fresh.append(norm(m.astype(F32), mod[3:4], mod[4:5]))
        for g in range(half // 8):
            both = jnp.concatenate([x[g * 8 : g * 8 + 8] for x in fresh], 0)
            tin[start + g * 16 : start + g * 16 + 16] = both.astype(BF)

    def table(i):
        rows = [jnp.broadcast_to(tab[2 * i + f : 2 * i + f + 1], (8, D)) for f in range(2)]
        return jnp.concatenate(rows, 0)[None]

    def temporal_part(start, count, part):
        r = dot(tin[start : start + count], wtq[:, part * D : (part + 1) * D])
        groups = count // 16
        r = r.astype(BF)
        if part == 2:
            return r.reshape(groups, 16, D)
        r = r.astype(F32)
        low = pltpu.roll(r, D - HD // 2, 1).reshape(groups, 16, D)
        high = pltpu.roll(r, HD // 2, 1).reshape(groups, 16, D)
        r = r.reshape(groups, 16, D)
        return (r * table(0) + low * table(1) + high * table(2)).astype(BF)

    def main_part(part, ref, group):
        return ref.at[group, :, pl.ds(part * D, D)]

    finish_spatial(0)
    for part in range(3):
        ts[:, :, part * D : (part + 1) * D] = temporal_part(0, 256, part)
        pltpu.make_async_copy(
            main_part(part, ts, fi), main_part(part, tr, fi), t_recv.at[part, fi]
        ).start()

        def send_main(k, _):
            peer = at_frame(k)
            remote(
                main_part(part, ts, peer), main_part(part, tr, fi),
                t_send.at[part, peer], t_recv.at[part, fi], (peer, hi),
            ).start()
            return 0

        lax.fori_loop(1, NF, send_main, 0)

    finish_spatial(1)
    for part in range(3):
        r = temporal_part(256, 128, part)
        tsh[:, 0, :, part * WIN : (part + 1) * WIN] = r[:, :, 0:WIN]
        tsh[:, 1, :, part * WIN : (part + 1) * WIN] = r[:, :, D - WIN : D]
    pltpu.make_async_copy(tsh.at[fi // 2, lax.rem(fi, 2)], trh.at[fi], th_recv.at[fi]).start()

    def send_half(k, _):
        peer = at_frame(k)
        remote(
            tsh.at[peer // 2, lax.rem(peer, 2)], trh.at[fi],
            th_send.at[peer], th_recv.at[fi], (peer, hi),
        ).start()
        return 0

    lax.fori_loop(1, NF, send_half, 0)

    window = lax.broadcasted_iota(jnp.int32, (256, 256), 1)

    def temporal_head(source, width, offset, total):
        tile = jnp.minimum(offset // 128, width // 128 - 2)
        begin = offset - tile * 128
        own = (window >= begin) & (window < begin + HD)

        def part(i):
            at = pl.multiple_of(i * width + tile * 128, 128)
            return source[:, :, pl.ds(at, 256)].reshape(256, 256)

        q = part(0)
        s = dot(jnp.where(own, q, jnp.zeros_like(q)), part(1), NT) + bias[...]
        e = jnp.exp2((s - jnp.max(s, axis=1, keepdims=True)) * SCALE)
        o = dot(e.astype(BF), part(2)) * (1.0 / jnp.sum(e, axis=1, keepdims=True))
        lanes = pl.ds(pl.multiple_of(tile * 128, 128), 256)
        total[:, lanes] = jnp.where(own, o, total[:, lanes])

    acc[...] = jnp.zeros_like(acc)
    acch[...] = jnp.zeros_like(acch)

    def arrive_main(k, _):
        src = at_frame(k)
        for part in range(3):
            await_bytes(main_part(part, tr, src), t_recv.at[part, src])
        return 0

    lax.fori_loop(0, NF, arrive_main, 0)

    def main_heads(j, _):
        for b in range(4):
            temporal_head(tr, D, (4 * j + b) * HD, acc)
        return 0

    lax.fori_loop(0, H // 4, main_heads, 0)
    to[...] = acc[...].astype(BF).reshape(NF, 16, D)
    pltpu.make_async_copy(to.at[fi], ro.at[fi], u_recv.at[fi]).start()

    def return_main(k, _):
        peer = at_frame(k)
        remote(to.at[peer], ro.at[fi], u_send.at[peer], u_recv.at[fi], (peer, hi)).start()
        return 0

    lax.fori_loop(1, NF, return_main, 0)

    def arrive_half(k, _):
        src = at_frame(k)
        await_bytes(trh.at[src], th_recv.at[src])
        return 0

    lax.fori_loop(0, NF, arrive_half, 0)

    def half_heads(j, _):
        for b in range(4):
            temporal_head(trh, WIN, (4 * j + b) * HD + 64 * lax.rem(fi, 2), acch)
        return 0

    lax.fori_loop(0, H // 8, half_heads, 0)
    toh[...] = acch[...].astype(BF).reshape(NF, 16, WIN)

    def half_place(src):
        return roh.at[lax.rem(src, 2), src // 2]

    pltpu.make_async_copy(toh.at[fi], half_place(fi), uh_recv.at[fi]).start()

    def return_half(k, _):
        peer = at_frame(k)
        remote(toh.at[peer], half_place(fi), uh_send.at[peer], uh_recv.at[fi], (peer, hi)).start()
        return 0

    lax.fori_loop(1, NF, return_half, 0)

    loads[7].wait()

    def finish(r, first, half):
        for f in range(2):
            for j in range(half // 16):
                at = 32 * j + 8 * f
                rows = jnp.concatenate([r[at : at + 8], r[at + 16 : at + 24]], 0)
                here = slice(first + 16 * j, first + 16 * j + 16)
                out[f, here] = (mid[f, here].astype(F32) + mod[5:6] * rows).astype(BF)

    def back_main(k, _):
        src = at_frame(k)
        await_bytes(ro.at[src], u_recv.at[src])
        return 0

    lax.fori_loop(0, NF, back_main, 0)
    finish(dot(ro[...].reshape(256, D), wto[...]), 0, 128)

    def back_half(k, _):
        src = at_frame(k)
        await_bytes(half_place(src), uh_recv.at[src])
        return 0

    lax.fori_loop(0, NF, back_half, 0)
    r = dot(roh[0].reshape(128, WIN), wto[0:WIN]) + dot(roh[1].reshape(128, WIN), wto[D - WIN : D])
    finish(r, 128, 64)

    def sent_head(k, _):
        peer = at_head(k)
        for kind in range(4):
            await_bytes(piece(kind, proj, peer), s_send.at[kind, peer])
        for kind, lanes in ((0, pl.ds(0, 256)), (1, pl.ds(256, 128))):
            await_bytes(ot.at[peer, :, lanes], r_send.at[kind, peer])
        return 0

    lax.fori_loop(1, NH, sent_head, 0)

    def sent_frame(k, _):
        peer = at_frame(k)
        for part in range(3):
            await_bytes(main_part(part, ts, peer), t_send.at[part, peer])
        await_bytes(trh.at[peer], th_send.at[peer])
        await_bytes(to.at[peer], u_send.at[peer])
        await_bytes(toh.at[peer], uh_send.at[peer])
        return 0

    lax.fori_loop(1, NF, sent_frame, 0)


def local(latents, modulation, spatial_qkv, spatial_out, temporal_qkv, temporal_out):
    anywhere = pl.BlockSpec(memory_space=pl.ANY)
    vmem = pl.BlockSpec(memory_space=pltpu.VMEM)
    dma = pltpu.SemaphoreType.DMA
    return pl.pallas_call(
        kernel,
        out_shape=jax.ShapeDtypeStruct((2, PATCH, D), BF),
        in_specs=[anywhere, vmem] + [anywhere] * 5,
        out_specs=vmem,
        scratch_shapes=[
            pltpu.VMEM((2, PATCH, D), BF),
            pltpu.VMEM((8, D), F32),
            pltpu.VMEM((D, 3 * D), BF),
            pltpu.VMEM((D, D), BF),
            pltpu.VMEM((D, 3 * D), BF),
            pltpu.VMEM((D, D), BF),
            dma((8,)),
            pltpu.VMEM((TOK, D), BF),
            pltpu.VMEM((3, NH, PAIR, TOK), BF),
            pltpu.VMEM((3, NH, PAIR, TOK), BF),
            pltpu.VMEM((2, PAIR, KEYS), BF),
            pltpu.VMEM((2, PAIR + 16, KEYS), BF),
            pltpu.VMEM((6, 2, 256, PAIR), BF),
            pltpu.VMEM((2, 256, KEYS), F32),
            pltpu.VMEM((2, 256, PAIR), BF),
            pltpu.VMEM((NH, PAIR, TOK), BF),
            pltpu.VMEM((NH, PAIR, TOK), BF),
            pltpu.VMEM((TOK, D), BF),
            pltpu.VMEM((2, PATCH, D), BF),
            pltpu.VMEM((TOK, D), BF),
            pltpu.VMEM((NF, 16, 3 * D), BF),
            pltpu.VMEM((8, 2, 16, 3 * WIN), BF),
            pltpu.VMEM((NF, 16, 3 * D), BF),
            pltpu.VMEM((NF, 16, 3 * WIN), BF),
            pltpu.VMEM((256, D), F32),
            pltpu.VMEM((256, WIN), F32),
            pltpu.VMEM((NF, 16, D), BF),
            pltpu.VMEM((NF, 16, WIN), BF),
            pltpu.VMEM((NF, 16, D), BF),
            pltpu.VMEM((2, 8, 16, WIN), BF),
            pltpu.VMEM((256, 256), F32),
            dma((4, NH)), dma((4, NH)), dma((2, NH)), dma((2, NH)),
            dma((3, NF)), dma((3, NF)), dma((NF,)), dma((NF,)),
            dma((NF,)), dma((NF,)), dma((NF,)), dma((NF,)),
        ],
        compiler_params=pltpu.CompilerParams(
            collective_id=0, has_side_effects=True, vmem_limit_bytes=62 * 2**20
        ),
    )(
        latents, modulation, jnp.asarray(rope_table()),
        spatial_qkv, spatial_out, temporal_qkv, temporal_out,
    )


def solution(mesh):
    return jax.shard_map(
        local,
        mesh=mesh,
        in_specs=(P("frame", "head", None), P(), P(), P(), P(), P()),
        out_specs=P("frame", "head", None),
        check_vma=False,
    )
```

```python
import math

import jax
import jax.numpy as jnp
import numpy as np
from jax import lax
from jax.experimental import pallas as pl
from jax.experimental.pallas import tpu as pltpu
from jax.sharding import PartitionSpec as P

MESH = pl.DeviceIdType.MESH
BF = jnp.bfloat16
F32 = jnp.float32
D, H, HD, F = 1152, 16, 72, 32
NH, NF = 8, 16
PAIR = 2 * HD
PATCH = 192
TOK = 2 * PATCH
KEYS = NH * PATCH
WIN = 5 * 128
SCALE = math.log2(math.e) / math.sqrt(HD)
NN = (((1,), (0,)), ((), ()))
NT = (((1,), (1,)), ((), ()))


def dot(a, b, dims=NN):
    return lax.dot_general(a, b, dims, preferred_element_type=F32)


def rope_table():
    inverse = 10000.0 ** (-np.arange(HD // 2) / (HD // 2))
    angles = np.arange(F)[:, None] * inverse[None, :]
    zeros = np.zeros_like(angles)
    cos = np.tile(np.concatenate([np.cos(angles)] * 2, 1), (1, H))
    low = np.tile(np.concatenate([-np.sin(angles), zeros], 1), (1, H))
    high = np.tile(np.concatenate([zeros, np.sin(angles)], 1), (1, H))
    rows = [np.concatenate([np.repeat(t, 8, 0), np.repeat(t, 4, 0)], 0) for t in (cos, low, high)]
    return np.stack(rows).astype(np.float32)


def norm(x, offset, stretch):
    centered = x - jnp.mean(x, axis=-1, keepdims=True)
    variance = jnp.mean(centered * centered, axis=-1, keepdims=True)
    return centered * lax.rsqrt(variance + 1e-06) * (1.0 + stretch) + offset


def kernel(
    lat_h, mod, tab_h, wsq_h, wso_h, wtq_h, wto_h, out,
    lat, tab, wsq, wso, wtq, wto, load_sem,
    nrm, proj, recv, ks, vs, qs, sc, ob, ot, orecv, oa,
    ts, tsh, tr, trh, mid, tin, tp, acc, to, toh, ro, roh, bias,
    s_send, s_recv, r_send, r_recv, t_send, t_recv, th_send, th_recv,
    u_send, u_recv, uh_send, uh_recv,
):
    fi, hi = lax.axis_index("frame"), lax.axis_index("head")

    def at_head(k):
        return lax.rem(hi + k, NH)

    def at_frame(k):
        return lax.rem(fi + k, NF)

    def load(src, dst, i):
        return pltpu.make_async_copy(src, dst, load_sem.at[i])

    part_loads = [
        load(wsq_h.at[:, pl.ds(p * D, D)], wsq.at[:, pl.ds(p * D, D)], 2 + p) for p in range(3)
    ]
    loads = [
        load(lat_h, lat, 0), load(tab_h, tab, 1), *part_loads,
        load(wso_h, wso, 5), load(wtq_h, wtq, 6), load(wto_h, wto, 7),
    ]
    for i in (0, 3, 4, 2):
        loads[i].start()

    barrier = pltpu.get_barrier_semaphore()

    def greet(k, _):
        pl.semaphore_signal(barrier, inc=1, device_id=(fi, at_head(k)), device_id_type=MESH)
        return 0

    def greet_frame(k, _):
        pl.semaphore_signal(barrier, inc=1, device_id=(at_frame(k), hi), device_id_type=MESH)
        return 0

    lax.fori_loop(1, NH, greet, 0)
    lax.fori_loop(1, NF, greet_frame, 0)

    def remote(src, dst, send, receive, device):
        return pltpu.make_async_remote_copy(
            src_ref=src, dst_ref=dst, send_sem=send, recv_sem=receive,
            device_id=device, device_id_type=MESH,
        )

    def await_bytes(ref, sem):
        pltpu.make_async_copy(ref, ref, sem).wait()

    loads[0].wait()
    for row, f, p, n in ((0, 0, 0, 192), (192, 1, 128, 64), (256, 1, 0, 128)):
        x = lat[f, p : p + n].astype(F32)
        nrm[row : row + n] = norm(x, mod[0:1], mod[1:2]).astype(BF)

    def piece(phase, ref, part, block):
        rows = (pl.ds(0, 80), pl.ds(80, 64))[phase % 2]
        lanes = (pl.ds(0, 256), pl.ds(256, 128))[phase // 2]
        return ref.at[part, block, rows, lanes]

    def spatial_send(phase, part):
        pltpu.make_async_copy(
            piece(phase, proj, part, hi), piece(phase, recv, part, hi), s_recv.at[phase, part, hi]
        ).start()

        def send(k, _):
            peer = at_head(k)
            remote(
                piece(phase, proj, part, peer), piece(phase, recv, part, hi),
                s_send.at[phase, part, peer], s_recv.at[phase, part, hi], (fi, peer),
            ).start()
            return 0

        lax.fori_loop(1, NH, send, 0)

    for slot, part in enumerate((1, 2, 0)):
        part_loads[part].wait()
        r = dot(nrm[...], wsq[:, part * D : (part + 1) * D])
        proj[slot] = r.astype(BF).T.reshape(NH, PAIR, TOK)
        if slot == 0:
            pl.semaphore_wait(barrier, NH + NF - 2)
        spatial_send(0, slot)
    for phase in range(1, 4):
        for slot in range(3):
            spatial_send(phase, slot)
    for i in (5, 6, 1, 7):
        loads[i].start()

    row = lax.broadcasted_iota(jnp.int32, (256, 256), 0)
    col = lax.broadcasted_iota(jnp.int32, (256, 256), 1)
    bias[0] = jnp.where(row % 8 == col % 8, 0.0, -jnp.inf).astype(F32)
    bias[1] = jnp.where(row % 4 == col % 4, 0.0, -jnp.inf).astype(F32)

    for rows in (slice(0, 16), slice(16 + PAIR, 32 + PAIR)):
        vs[:, rows, :] = jnp.ones((2, 16, KEYS), BF)

    def halves(a, b):
        a, b = a.astype(F32), b.astype(F32)
        lane = lax.broadcasted_iota(jnp.int32, a.shape, 1)
        first = jnp.where(lane < 64, a, pltpu.roll(b, 64, 1))
        second = jnp.where(lane < 64, pltpu.roll(a, 64, 1), b)
        return first.astype(BF), second.astype(BF)

    def prepare(f, h):
        phase = 2 * f + h
        lo, n = ((0, 80), (80, 64))[h]
        own = lax.broadcasted_iota(jnp.int32, (128, 80), 1)
        own = (own < HD) if h == 0 else (own >= 80 - HD)

        def body(j, _):
            sources = (2 * j, 2 * j + 1)
            for src in sources:
                for part in range(3):
                    await_bytes(piece(phase, recv, part, src), s_recv.at[phase, part, src])
            for part, ref, up in ((0, ks, 0), (1, vs, 16)):
                for src in sources:
                    at = pl.multiple_of(src * 128, 128)
                    lanes = slice(0, 128) if f == 0 else slice(256, 384)
                    ref[f, lo + up : lo + up + n, pl.ds(at, 128)] = recv[part, src, lo : lo + n, lanes]
                if f == 0:
                    at = pl.multiple_of(1024 + j * 128, 128)
                    tiles = halves(*(recv[part, src, lo : lo + n, 128:256] for src in sources))
                    for g in range(2):
                        ref[g, lo + up : lo + up + n, pl.ds(at, 128)] = tiles[g]
            for i, src in enumerate(sources):
                rows = slice(64 * h, 64 * h + 80)
                lanes = slice(0, 128) if f == 0 else slice(256, 384)
                q = recv[2, src, rows, lanes].T
                qs[j, i * 128 : i * 128 + 128] = jnp.where(own, q, jnp.zeros_like(q))
                q = recv[2, src, rows, 128:256].T[f * 64 : f * 64 + 64]
                q = jnp.where(own[0:64], q, jnp.zeros_like(q))
                qs[4 + j // 2, pl.ds(pl.multiple_of(j % 2 * 128 + i * 64, 64), 64)] = q
            return 0

        lax.fori_loop(0, NH // 2, body, 0)

    def scores(b, f, h):
        return dot(qs[b], ks[f, 64 * h : 64 * h + 80])

    def mixed(s, f, h):
        p = jnp.exp2((s - jnp.max(s, axis=1, keepdims=True)) * SCALE).astype(BF)
        o = dot(p, vs[f, 80 * h : 80 * h + 96], NT)
        one = 80 * h
        return (o * (1.0 / o[:, one : one + 1])).astype(BF)

    def back_piece(kind, ref, block):
        rows = (pl.ds(0, 64), pl.ds(64, 80))[kind % 2]
        return ref.at[block, rows, pl.ds(kind // 2 * 128, 128)]

    def give(kind, src):
        here, there = back_piece(kind, ot, src), back_piece(kind, orecv, hi)

        @pl.when(src == hi)
        def _():
            pltpu.make_async_copy(here, there, r_recv.at[kind, hi]).start()

        @pl.when(src != hi)
        def _():
            remote(here, there, r_send.at[kind, src], r_recv.at[kind, hi], (fi, src)).start()

    def put(src, h, lanes, o):
        if h == 0:
            ot[src, 0:80, lanes] = o[16:96]
        else:
            row = lax.broadcasted_iota(jnp.int32, (16, o.shape[1]), 0)
            ot[src, 64:80, lanes] = jnp.where(row < 8, ot[src, 64:80, lanes], o[0:16])
            ot[src, 80:PAIR, lanes] = o[16:80]

    def attend(f, h):
        prepare(f, h)
        sc[0] = scores(0, f, h)

        def body(j, _):
            for u in range(2):
                s = sc[u]
                sc[1 - u] = scores(jnp.minimum(2 * j + u + 1, 5), f, h)
                ob[u] = mixed(s, f, h)

            @pl.when(j < 2)
            def _():
                for u in range(2):
                    o = ob[u].T
                    for i in range(2):
                        src = 2 * (2 * j + u) + i
                        lanes = slice(0, 128) if f == 0 else slice(256, 384)
                        put(src, h, lanes, o[:, i * 128 : i * 128 + 128])
                        give(4 * f + h, src)

            @pl.when(j == 2)
            def _():
                for u in range(2):
                    for i in range(4):
                        src = 4 * u + i
                        o = ob[u, i * 64 : i * 64 + 64].T
                        put(src, h, slice(128 + 64 * f, 192 + 64 * f), o)
                        if f == 1:
                            give(2 + h, src)

            return 0

        lax.fori_loop(0, 3, body, 0)

    for f in range(2):
        for h in range(2):
            attend(f, h)

    for i in (1, 5):
        loads[i].wait()
    sub = lax.broadcasted_iota(jnp.int32, (8, D), 0)

    def swap(a, b):
        first = jnp.where(sub < 4, a, pltpu.roll(b, 4, 0))
        second = jnp.where(sub < 4, pltpu.roll(a, 4, 0), b)
        return first, second

    def pack(x):
        return jnp.concatenate([x[:, 0:WIN], x[:, D - WIN : D]], 0).astype(BF)

    def unpack(x):
        x = x.astype(F32)
        return jnp.concatenate([x[0:8], x[8:16, 2 * WIN - D : WIN]], 1)

    def finish_spatial(kind):
        kinds = ((0, 1, 4, 5), (2, 3))[kind]

        def arrive(src, _):
            for one in kinds:
                await_bytes(back_piece(one, orecv, src), r_recv.at[one, src])
            return 0

        lax.fori_loop(0, NH, arrive, 0)
        start, count = ((0, 256), (256, 128))[kind]
        for t, at in enumerate(((0, 256), (128,))[kind]):
            row = start + t * 128
            oa[row : row + 128] = orecv[:, :, at : at + 128].reshape(D, 128).T
        r = dot(oa[start : start + count], wso[...])
        half = count // 2
        first = 128 * kind
        fresh = []
        for f in range(2):
            x = lat[f, first : first + half].astype(F32)
            fresh.append(x + mod[2:3] * r[f * half : (f + 1) * half])
        for g in range(half // 8):
            a, b = (x[g * 8 : g * 8 + 8] for x in fresh)
            if kind == 0:
                ts[g] = jnp.concatenate([a, b], 0).astype(BF)
            else:
                a, b = swap(a, b)
                tsh[2 * g], tsh[2 * g + 1] = pack(a), pack(b)

    def exchange(source, target, send, receive):
        pltpu.make_async_copy(source.at[fi], target.at[fi], receive.at[fi]).start()

        def one(k, _):
            peer = at_frame(k)
            remote(
                source.at[peer], target.at[fi], send.at[peer], receive.at[fi], (peer, hi)
            ).start()
            return 0

        lax.fori_loop(1, NF, one, 0)

    def arrived(target, receive):
        def one(k, _):
            src = at_frame(k)
            await_bytes(target.at[src], receive.at[src])
            return 0

        lax.fori_loop(0, NF, one, 0)

    finish_spatial(0)
    exchange(ts, tr, t_send, t_recv)
    finish_spatial(1)
    exchange(tsh, trh, th_send, th_recv)

    def temporal_project(start, count):
        rows = slice(start, start + count)
        tin[rows] = norm(mid[rows], mod[3:4], mod[4:5]).astype(BF)
        for part in range(3):
            r = dot(tin[rows], wtq[:, part * D : (part + 1) * D]).astype(BF)
            if part < 2:
                r = r.astype(F32)
                low = pltpu.roll(r, D - HD // 2, 1)
                high = pltpu.roll(r, HD // 2, 1)
                r = (r * tab[0, rows] + low * tab[1, rows] + high * tab[2, rows]).astype(BF)
            tp[rows, part * D : (part + 1) * D] = r

    def temporal_head(start, count, offset):
        rows = slice(start, start + count)
        tile = jnp.minimum(offset // 128, 7)
        begin = offset - tile * 128
        lane = lax.broadcasted_iota(jnp.int32, (count, 256), 1)
        own = (lane >= begin) & (lane < begin + HD)

        def part(i):
            return tp[rows, pl.ds(pl.multiple_of(i * D + tile * 128, 128), 256)]

        q = part(0)
        s = dot(jnp.where(own, q, jnp.zeros_like(q)), part(1), NT)
        s = s + bias[0 if count == 256 else 1, 0:count, 0:count]
        e = jnp.exp2((s - jnp.max(s, axis=1, keepdims=True)) * SCALE)
        o = dot(e.astype(BF), part(2)) * (1.0 / jnp.sum(e, axis=1, keepdims=True))
        lanes = pl.ds(pl.multiple_of(tile * 128, 128), 256)
        acc[rows, lanes] = jnp.where(own, o, acc[rows, lanes])

    def temporal_attend(start, count):
        def heads(j, _):
            for b in range(4):
                temporal_head(start, count, (4 * j + b) * HD)
            return 0

        lax.fori_loop(0, H // 4, heads, 0)
        rows = slice(start, start + count)
        return mid[rows] + mod[5:6] * dot(acc[rows].astype(BF), wto[...])

    acc[...] = jnp.zeros_like(acc)
    for i in (6, 7):
        loads[i].wait()
    arrived(tr, t_recv)
    mid[0:256] = tr[...].reshape(256, D).astype(F32)
    temporal_project(0, 256)
    to[...] = temporal_attend(0, 256).astype(BF).reshape(NF, 16, D)
    exchange(to, ro, u_send, u_recv)

    arrived(trh, th_recv)
    for j in range(NF):
        mid[256 + j * 8 : 264 + j * 8] = unpack(trh[j])
    temporal_project(256, 128)
    r = temporal_attend(256, 128)
    for j in range(NF):
        toh[j] = pack(r[j * 8 : j * 8 + 8])
    exchange(toh, roh, uh_send, uh_recv)

    arrived(ro, u_recv)
    for j in range(NF // 2):
        a, b = ro[2 * j].astype(F32), ro[2 * j + 1].astype(F32)
        for f in range(2):
            rows = jnp.concatenate([a[f * 8 : f * 8 + 8], b[f * 8 : f * 8 + 8]], 0)
            out[f, 16 * j : 16 * j + 16] = rows.astype(BF)
    arrived(roh, uh_recv)
    for j in range(NF // 4):
        a, b = (swap(unpack(roh[4 * j + i]), unpack(roh[4 * j + i + 1])) for i in (0, 2))
        for f in range(2):
            rows = jnp.concatenate([a[f], b[f]], 0)
            out[f, 128 + 16 * j : 144 + 16 * j] = rows.astype(BF)

    def sent_head(k, _):
        peer = at_head(k)
        for phase in range(4):
            for part in range(3):
                await_bytes(piece(phase, proj, part, peer), s_send.at[phase, part, peer])
        for kind in range(6):
            await_bytes(back_piece(kind, ot, peer), r_send.at[kind, peer])
        return 0

    lax.fori_loop(1, NH, sent_head, 0)

    def sent_frame(k, _):
        peer = at_frame(k)
        await_bytes(ts.at[peer], t_send.at[peer])
        await_bytes(tsh.at[peer], th_send.at[peer])
        await_bytes(to.at[peer], u_send.at[peer])
        await_bytes(toh.at[peer], uh_send.at[peer])
        return 0

    lax.fori_loop(1, NF, sent_frame, 0)


def local(latents, modulation, spatial_qkv, spatial_out, temporal_qkv, temporal_out):
    anywhere = pl.BlockSpec(memory_space=pl.ANY)
    vmem = pl.BlockSpec(memory_space=pltpu.VMEM)
    dma = pltpu.SemaphoreType.DMA
    return pl.pallas_call(
        kernel,
        out_shape=jax.ShapeDtypeStruct((2, PATCH, D), BF),
        in_specs=[anywhere, vmem] + [anywhere] * 5,
        out_specs=vmem,
        scratch_shapes=[
            pltpu.VMEM((2, PATCH, D), BF),
            pltpu.VMEM((3, TOK, D), F32),
            pltpu.VMEM((D, 3 * D), BF),
            pltpu.VMEM((D, D), BF),
            pltpu.VMEM((D, 3 * D), BF),
            pltpu.VMEM((D, D), BF),
            dma((8,)),
            pltpu.VMEM((TOK, D), BF),
            pltpu.VMEM((3, NH, PAIR, TOK), BF),
            pltpu.VMEM((3, NH, PAIR, TOK), BF),
            pltpu.VMEM((2, PAIR, KEYS), BF),
            pltpu.VMEM((2, PAIR + 32, KEYS), BF),
            pltpu.VMEM((6, 256, 80), BF),
            pltpu.VMEM((2, 256, KEYS), F32),
            pltpu.VMEM((2, 256, 96), BF),
            pltpu.VMEM((NH, PAIR, TOK), BF),
            pltpu.VMEM((NH, PAIR, TOK), BF),
            pltpu.VMEM((TOK, D), BF),
            pltpu.VMEM((NF, 16, D), BF),
            pltpu.VMEM((NF, 16, WIN), BF),
            pltpu.VMEM((NF, 16, D), BF),
            pltpu.VMEM((NF, 16, WIN), BF),
            pltpu.VMEM((TOK, D), F32),
            pltpu.VMEM((TOK, D), BF),
            pltpu.VMEM((TOK, 3 * D), BF),
            pltpu.VMEM((TOK, D), F32),
            pltpu.VMEM((NF, 16, D), BF),
            pltpu.VMEM((NF, 16, WIN), BF),
            pltpu.VMEM((NF, 16, D), BF),
            pltpu.VMEM((NF, 16, WIN), BF),
            pltpu.VMEM((2, 256, 256), F32),
            dma((4, 3, NH)), dma((4, 3, NH)), dma((6, NH)), dma((6, NH)),
            dma((NF,)), dma((NF,)), dma((NF,)), dma((NF,)),
            dma((NF,)), dma((NF,)), dma((NF,)), dma((NF,)),
        ],
        compiler_params=pltpu.CompilerParams(
            collective_id=0, has_side_effects=True, vmem_limit_bytes=62 * 2**20
        ),
    )(
        latents, modulation, jnp.asarray(rope_table()),
        spatial_qkv, spatial_out, temporal_qkv, temporal_out,
    )


def solution(mesh):
    return jax.shard_map(
        local,
        mesh=mesh,
        in_specs=(P("frame", "head", None), P(), P(), P(), P(), P()),
        out_specs=P("frame", "head", None),
        check_vma=False,
    )
```

```python
import math

import jax
import jax.numpy as jnp
import numpy as np
from jax import lax
from jax.experimental import pallas as pl
from jax.experimental.pallas import tpu as pltpu
from jax.sharding import PartitionSpec as P

MESH = pl.DeviceIdType.MESH
BF = jnp.bfloat16
F32 = jnp.float32
D, H, HD, F = 1152, 16, 72, 32
NH, NF = 8, 16
PAIR = 2 * HD
PATCH = 192
TOK = 2 * PATCH
KEYS = NH * PATCH
WIN = 5 * 128
SCALE = math.log2(math.e) / math.sqrt(HD)
NN = (((1,), (0,)), ((), ()))
NT = (((1,), (1,)), ((), ()))


def dot(a, b, dims=NN):
    return lax.dot_general(a, b, dims, preferred_element_type=F32)


def rope_table():
    inverse = 10000.0 ** (-np.arange(HD // 2) / (HD // 2))
    angles = np.arange(F)[:, None] * inverse[None, :]
    zeros = np.zeros_like(angles)
    cos = np.tile(np.concatenate([np.cos(angles)] * 2, 1), (1, H))
    low = np.tile(np.concatenate([-np.sin(angles), zeros], 1), (1, H))
    high = np.tile(np.concatenate([zeros, np.sin(angles)], 1), (1, H))
    rows = [
        np.concatenate([np.repeat(t[0::2], 8, 0), np.repeat(t[1::2], 8, 0), np.repeat(t, 4, 0)], 0)
        for t in (cos, low, high)
    ]
    return np.stack(rows).astype(np.float32)


def norm(x, offset, stretch):
    centered = x - jnp.mean(x, axis=-1, keepdims=True)
    variance = jnp.mean(centered * centered, axis=-1, keepdims=True)
    return centered * lax.rsqrt(variance + 1e-06) * (1.0 + stretch) + offset


def kernel(
    lat_h, mod, tab_h, wsq_h, wso_h, wtq_h, wto_h, out,
    lat, tab, wsq, wso, wtq, wto, load_sem,
    nrm, proj, recv, ks, vs, qs, sc, ob, ot, orecv, oa,
    ts, tr, mid, tin, tp, acc, to, toh, ro, roh, bias,
    s_send, s_recv, r_send, r_recv, t_send, t_recv,
    u_send, u_recv, uh_send, uh_recv,
):
    fi, hi = lax.axis_index("frame"), lax.axis_index("head")

    def at_head(k):
        return lax.rem(hi + k, NH)

    def at_frame(k):
        return lax.rem(fi + k, NF)

    def load(src, dst, i):
        return pltpu.make_async_copy(src, dst, load_sem.at[i])

    part_loads = [
        load(wsq_h.at[:, pl.ds(p * D, D)], wsq.at[:, pl.ds(p * D, D)], 2 + p) for p in range(3)
    ]
    loads = [
        load(lat_h, lat, 0), load(tab_h, tab, 1), *part_loads,
        load(wso_h, wso, 5), load(wtq_h, wtq, 6), load(wto_h, wto, 7),
    ]
    for i in (0, 3, 4, 2):
        loads[i].start()

    barrier = pltpu.get_barrier_semaphore()

    def greet(k, _):
        pl.semaphore_signal(barrier, inc=1, device_id=(fi, at_head(k)), device_id_type=MESH)
        return 0

    def greet_frame(k, _):
        pl.semaphore_signal(barrier, inc=1, device_id=(at_frame(k), hi), device_id_type=MESH)
        return 0

    lax.fori_loop(1, NH, greet, 0)
    lax.fori_loop(1, NF, greet_frame, 0)

    def remote(src, dst, send, receive, device):
        return pltpu.make_async_remote_copy(
            src_ref=src, dst_ref=dst, send_sem=send, recv_sem=receive,
            device_id=device, device_id_type=MESH,
        )

    def await_bytes(ref, sem):
        pltpu.make_async_copy(ref, ref, sem).wait()

    loads[0].wait()
    for row, f, p, n in ((0, 0, 0, 192), (192, 1, 128, 64), (256, 1, 0, 128)):
        x = lat[f, p : p + n].astype(F32)
        nrm[row : row + n] = norm(x, mod[0:1], mod[1:2]).astype(BF)

    def piece(phase, ref, part, block):
        rows = (pl.ds(0, 80), pl.ds(80, 64))[phase % 2]
        lanes = (pl.ds(0, 256), pl.ds(256, 128))[phase // 2]
        return ref.at[part, block, rows, lanes]

    def spatial_send(phase, part):
        pltpu.make_async_copy(
            piece(phase, proj, part, hi), piece(phase, recv, part, hi), s_recv.at[phase, part, hi]
        ).start()

        def send(k, _):
            peer = at_head(k)
            remote(
                piece(phase, proj, part, peer), piece(phase, recv, part, hi),
                s_send.at[phase, part, peer], s_recv.at[phase, part, hi], (fi, peer),
            ).start()
            return 0

        lax.fori_loop(1, NH, send, 0)

    for slot, part in enumerate((1, 2, 0)):
        part_loads[part].wait()
        r = dot(nrm[...], wsq[:, part * D : (part + 1) * D])
        proj[slot] = r.astype(BF).T.reshape(NH, PAIR, TOK)
        if slot == 0:
            pl.semaphore_wait(barrier, NH + NF - 2)
        spatial_send(0, slot)
    for phase in range(1, 4):
        for slot in range(3):
            spatial_send(phase, slot)
    for i in (5, 6, 1, 7):
        loads[i].start()

    row = lax.broadcasted_iota(jnp.int32, (256, 256), 0)
    col = lax.broadcasted_iota(jnp.int32, (256, 256), 1)
    bias[0] = jnp.where(row % 8 == col % 8, 0.0, -jnp.inf).astype(F32)
    bias[1] = jnp.where(row % 4 == col % 4, 0.0, -jnp.inf).astype(F32)

    for rows in (slice(0, 16), slice(16 + PAIR, 32 + PAIR)):
        vs[:, rows, :] = jnp.ones((2, 16, KEYS), BF)

    def halves(a, b):
        a, b = a.astype(F32), b.astype(F32)
        lane = lax.broadcasted_iota(jnp.int32, a.shape, 1)
        first = jnp.where(lane < 64, a, pltpu.roll(b, 64, 1))
        second = jnp.where(lane < 64, pltpu.roll(a, 64, 1), b)
        return first.astype(BF), second.astype(BF)

    def prepare(f, h):
        phase = 2 * f + h
        lo, n = ((0, 80), (80, 64))[h]
        own = lax.broadcasted_iota(jnp.int32, (128, 80), 1)
        own = (own < HD) if h == 0 else (own >= 80 - HD)

        def body(j, _):
            sources = (2 * j, 2 * j + 1)
            for src in sources:
                for part in range(3):
                    await_bytes(piece(phase, recv, part, src), s_recv.at[phase, part, src])
            for part, ref, up in ((0, ks, 0), (1, vs, 16)):
                for src in sources:
                    at = pl.multiple_of(src * 128, 128)
                    lanes = slice(0, 128) if f == 0 else slice(256, 384)
                    ref[f, lo + up : lo + up + n, pl.ds(at, 128)] = recv[part, src, lo : lo + n, lanes]
                if f == 0:
                    at = pl.multiple_of(1024 + j * 128, 128)
                    tiles = halves(*(recv[part, src, lo : lo + n, 128:256] for src in sources))
                    for g in range(2):
                        ref[g, lo + up : lo + up + n, pl.ds(at, 128)] = tiles[g]
            for i, src in enumerate(sources):
                rows = slice(64 * h, 64 * h + 80)
                lanes = slice(0, 128) if f == 0 else slice(256, 384)
                q = recv[2, src, rows, lanes].T
                qs[j, i * 128 : i * 128 + 128] = jnp.where(own, q, jnp.zeros_like(q))
                q = recv[2, src, rows, 128:256].T[f * 64 : f * 64 + 64]
                q = jnp.where(own[0:64], q, jnp.zeros_like(q))
                qs[4 + j // 2, pl.ds(pl.multiple_of(j % 2 * 128 + i * 64, 64), 64)] = q
            return 0

        lax.fori_loop(0, NH // 2, body, 0)

    def scores(b, f, h):
        return dot(qs[b], ks[f, 64 * h : 64 * h + 80])

    def mixed(s, f, h):
        p = jnp.exp2((s - jnp.max(s, axis=1, keepdims=True)) * SCALE).astype(BF)
        o = dot(p, vs[f, 80 * h : 80 * h + 96], NT)
        one = 80 * h
        return (o * (1.0 / o[:, one : one + 1])).astype(BF)

    def back_piece(kind, ref, block):
        rows = (pl.ds(0, 64), pl.ds(64, 80))[kind % 2]
        return ref.at[block, rows, pl.ds(kind // 2 * 128, 128)]

    def give(kind, src):
        here, there = back_piece(kind, ot, src), back_piece(kind, orecv, hi)

        @pl.when(src == hi)
        def _():
            pltpu.make_async_copy(here, there, r_recv.at[kind, hi]).start()

        @pl.when(src != hi)
        def _():
            remote(here, there, r_send.at[kind, src], r_recv.at[kind, hi], (fi, src)).start()

    def put(src, h, lanes, o):
        if h == 0:
            ot[src, 0:80, lanes] = o[16:96]
        else:
            row = lax.broadcasted_iota(jnp.int32, (16, o.shape[1]), 0)
            ot[src, 64:80, lanes] = jnp.where(row < 8, ot[src, 64:80, lanes], o[0:16])
            ot[src, 80:PAIR, lanes] = o[16:80]

    def attend(f, h):
        prepare(f, h)
        sc[0] = scores(0, f, h)

        def body(j, _):
            for u in range(2):
                s = sc[u]
                sc[1 - u] = scores(jnp.minimum(2 * j + u + 1, 5), f, h)
                ob[u] = mixed(s, f, h)

            @pl.when(j < 2)
            def _():
                for u in range(2):
                    o = ob[u].T
                    for i in range(2):
                        src = 2 * (2 * j + u) + i
                        lanes = slice(0, 128) if f == 0 else slice(256, 384)
                        put(src, h, lanes, o[:, i * 128 : i * 128 + 128])
                        give(4 * f + h, src)

            @pl.when(j == 2)
            def _():
                for u in range(2):
                    for i in range(4):
                        src = 4 * u + i
                        o = ob[u, i * 64 : i * 64 + 64].T
                        put(src, h, slice(128 + 64 * f, 192 + 64 * f), o)
                        if f == 1:
                            give(2 + h, src)

            return 0

        lax.fori_loop(0, 3, body, 0)

    sub = lax.broadcasted_iota(jnp.int32, (8, D), 0)

    def swap(a, b):
        first = jnp.where(sub < 4, a, pltpu.roll(b, 4, 0))
        second = jnp.where(sub < 4, pltpu.roll(a, 4, 0), b)
        return first, second

    def pack(x):
        return jnp.concatenate([x[:, 0:WIN], x[:, D - WIN : D]], 0).astype(BF)

    def unpack(x):
        x = x.astype(F32)
        return jnp.concatenate([x[0:8], x[8:16, 2 * WIN - D : WIN]], 1)

    def finish_spatial(kind):
        tile = (0, 2, 1)[kind]

        def arrive(src, _):
            for h in range(2):
                await_bytes(back_piece(2 * tile + h, orecv, src), r_recv.at[2 * tile + h, src])
            return 0

        lax.fori_loop(0, NH, arrive, 0)
        rows = slice(kind * 128, kind * 128 + 128)
        oa[rows] = orecv[:, :, tile * 128 : tile * 128 + 128].reshape(D, 128).T
        r = mod[2:3] * dot(oa[rows], wso[...])
        if kind < 2:
            r = lat[kind, 0:128].astype(F32) + r
            for g in range(NF):
                ts[kind, g] = pack(r[g * 8 : g * 8 + 8])
        else:
            x = [lat[f, 128:PATCH].astype(F32) + r[f * 64 : f * 64 + 64] for f in range(2)]
            for g in range(NF // 2):
                a, b = swap(*(y[g * 8 : g * 8 + 8] for y in x))
                ts[2, 2 * g], ts[2, 2 * g + 1] = pack(a), pack(b)

    def exchange(source, target, send, receive):
        pltpu.make_async_copy(source.at[fi], target.at[fi], receive.at[fi]).start()

        def one(k, _):
            peer = at_frame(k)
            remote(
                source.at[peer], target.at[fi], send.at[peer], receive.at[fi], (peer, hi)
            ).start()
            return 0

        lax.fori_loop(1, NF, one, 0)

    def arrived(target, receive):
        def one(k, _):
            src = at_frame(k)
            await_bytes(target.at[src], receive.at[src])
            return 0

        lax.fori_loop(0, NF, one, 0)

    def temporal_project(start, count):
        rows = slice(start, start + count)
        tin[rows] = norm(mid[rows], mod[3:4], mod[4:5]).astype(BF)
        for part in range(3):
            r = dot(tin[rows], wtq[:, part * D : (part + 1) * D]).astype(BF)
            if part < 2:
                r = r.astype(F32)
                low = pltpu.roll(r, D - HD // 2, 1)
                high = pltpu.roll(r, HD // 2, 1)
                r = (r * tab[0, rows] + low * tab[1, rows] + high * tab[2, rows]).astype(BF)
            tp[rows, part * D : (part + 1) * D] = r

    def temporal_head(start, count, offset):
        rows = slice(start, start + count)
        tile = jnp.minimum(offset // 128, 7)
        begin = offset - tile * 128
        lane = lax.broadcasted_iota(jnp.int32, (count, 256), 1)
        own = (lane >= begin) & (lane < begin + HD)

        def part(i):
            return tp[rows, pl.ds(pl.multiple_of(i * D + tile * 128, 128), 256)]

        q = part(0)
        s = dot(jnp.where(own, q, jnp.zeros_like(q)), part(1), NT)
        s = s + bias[0 if count == 256 else 1, 0:count, 0:count]
        e = jnp.exp2((s - jnp.max(s, axis=1, keepdims=True)) * SCALE)
        o = dot(e.astype(BF), part(2)) * (1.0 / jnp.sum(e, axis=1, keepdims=True))
        return own, o, pl.ds(pl.multiple_of(tile * 128, 128), 256)

    def temporal_attend(start, count):
        group = 4 if count == 256 else 8
        rows = slice(start, start + count)

        def heads(j, _):
            done = [temporal_head(start, count, (group * j + b) * HD) for b in range(group)]
            for own, o, lanes in done:
                acc[rows, lanes] = jnp.where(own, o, acc[rows, lanes])
            return 0

        lax.fori_loop(0, H // group, heads, 0)
        return mid[rows] + mod[5:6] * dot(acc[rows].astype(BF), wto[...])

    def give_piece(kind):
        finish_spatial(kind)
        exchange(ts.at[kind], tr.at[kind], t_send.at[kind], t_recv.at[kind])

    def take_piece(kind):
        arrived(tr.at[kind], t_recv.at[kind])
        for j in range(NF):
            mid[kind * 128 + j * 8 : kind * 128 + j * 8 + 8] = unpack(tr[kind, j])
        temporal_project(kind * 128, 128)

    attend(0, 0)
    attend(0, 1)
    attend(1, 0)
    for i in (1, 5):
        loads[i].wait()
    give_piece(0)
    attend(1, 1)
    give_piece(1)
    give_piece(2)
    acc[...] = jnp.zeros_like(acc)
    for i in (6, 7):
        loads[i].wait()
    take_piece(0)
    take_piece(1)
    r = temporal_attend(0, 256)
    for j in range(NF):
        both = [r[f * 128 + j * 8 : f * 128 + j * 8 + 8] for f in range(2)]
        to[j] = jnp.concatenate(both, 0).astype(BF)
    exchange(to, ro, u_send, u_recv)
    take_piece(2)
    r = temporal_attend(256, 128)
    for j in range(NF):
        toh[j] = pack(r[j * 8 : j * 8 + 8])
    exchange(toh, roh, uh_send, uh_recv)

    arrived(ro, u_recv)
    for j in range(NF // 2):
        a, b = ro[2 * j].astype(F32), ro[2 * j + 1].astype(F32)
        for f in range(2):
            rows = jnp.concatenate([a[f * 8 : f * 8 + 8], b[f * 8 : f * 8 + 8]], 0)
            out[f, 16 * j : 16 * j + 16] = rows.astype(BF)
    arrived(roh, uh_recv)
    for j in range(NF // 4):
        a, b = (swap(unpack(roh[4 * j + i]), unpack(roh[4 * j + i + 1])) for i in (0, 2))
        for f in range(2):
            rows = jnp.concatenate([a[f], b[f]], 0)
            out[f, 128 + 16 * j : 144 + 16 * j] = rows.astype(BF)

    def sent_head(k, _):
        peer = at_head(k)
        for phase in range(4):
            for part in range(3):
                await_bytes(piece(phase, proj, part, peer), s_send.at[phase, part, peer])
        for kind in range(6):
            await_bytes(back_piece(kind, ot, peer), r_send.at[kind, peer])
        return 0

    lax.fori_loop(1, NH, sent_head, 0)

    def sent_frame(k, _):
        peer = at_frame(k)
        for kind in range(3):
            await_bytes(ts.at[kind, peer], t_send.at[kind, peer])
        await_bytes(to.at[peer], u_send.at[peer])
        await_bytes(toh.at[peer], uh_send.at[peer])
        return 0

    lax.fori_loop(1, NF, sent_frame, 0)


def local(latents, modulation, spatial_qkv, spatial_out, temporal_qkv, temporal_out):
    anywhere = pl.BlockSpec(memory_space=pl.ANY)
    vmem = pl.BlockSpec(memory_space=pltpu.VMEM)
    dma = pltpu.SemaphoreType.DMA
    return pl.pallas_call(
        kernel,
        out_shape=jax.ShapeDtypeStruct((2, PATCH, D), BF),
        in_specs=[anywhere, vmem] + [anywhere] * 5,
        out_specs=vmem,
        scratch_shapes=[
            pltpu.VMEM((2, PATCH, D), BF),
            pltpu.VMEM((3, TOK, D), F32),
            pltpu.VMEM((D, 3 * D), BF),
            pltpu.VMEM((D, D), BF),
            pltpu.VMEM((D, 3 * D), BF),
            pltpu.VMEM((D, D), BF),
            dma((8,)),
            pltpu.VMEM((TOK, D), BF),
            pltpu.VMEM((3, NH, PAIR, TOK), BF),
            pltpu.VMEM((3, NH, PAIR, TOK), BF),
            pltpu.VMEM((2, PAIR, KEYS), BF),
            pltpu.VMEM((2, PAIR + 32, KEYS), BF),
            pltpu.VMEM((6, 256, 80), BF),
            pltpu.VMEM((2, 256, KEYS), F32),
            pltpu.VMEM((2, 256, 96), BF),
            pltpu.VMEM((NH, PAIR, TOK), BF),
            pltpu.VMEM((NH, PAIR, TOK), BF),
            pltpu.VMEM((TOK, D), BF),
            pltpu.VMEM((3, NF, 16, WIN), BF),
            pltpu.VMEM((3, NF, 16, WIN), BF),
            pltpu.VMEM((TOK, D), F32),
            pltpu.VMEM((TOK, D), BF),
            pltpu.VMEM((TOK, 3 * D), BF),
            pltpu.VMEM((TOK, D), F32),
            pltpu.VMEM((NF, 16, D), BF),
            pltpu.VMEM((NF, 16, WIN), BF),
            pltpu.VMEM((NF, 16, D), BF),
            pltpu.VMEM((NF, 16, WIN), BF),
            pltpu.VMEM((2, 256, 256), F32),
            dma((4, 3, NH)), dma((4, 3, NH)), dma((6, NH)), dma((6, NH)),
            dma((3, NF)), dma((3, NF)), dma((NF,)), dma((NF,)),
            dma((NF,)), dma((NF,)),
        ],
        compiler_params=pltpu.CompilerParams(
            collective_id=0, has_side_effects=True, vmem_limit_bytes=62 * 2**20
        ),
    )(
        latents, modulation, jnp.asarray(rope_table()),
        spatial_qkv, spatial_out, temporal_qkv, temporal_out,
    )


def solution(mesh):
    return jax.shard_map(
        local,
        mesh=mesh,
        in_specs=(P("frame", "head", None), P(), P(), P(), P(), P()),
        out_specs=P("frame", "head", None),
        check_vma=False,
    )
```

```python
import math

import jax
import jax.numpy as jnp
import numpy as np
from jax import lax
from jax.experimental import pallas as pl
from jax.experimental.pallas import tpu as pltpu
from jax.sharding import PartitionSpec as P

MESH = pl.DeviceIdType.MESH
BF = jnp.bfloat16
F32 = jnp.float32
D, H, HD, F = 1152, 16, 72, 32
NH, NF = 8, 16
PAIR = 2 * HD
PATCH = 192
TOK = 2 * PATCH
KEYS = NH * PATCH
WIN = 5 * 128
SCALE = math.log2(math.e) / math.sqrt(HD)
NN = (((1,), (0,)), ((), ()))
NT = (((1,), (1,)), ((), ()))


def dot(a, b, dims=NN):
    return lax.dot_general(a, b, dims, preferred_element_type=F32)


def rope_table():
    inverse = 10000.0 ** (-np.arange(HD // 2) / (HD // 2))
    angles = np.arange(F)[:, None] * inverse[None, :]
    zeros = np.zeros_like(angles)
    cos = np.tile(np.concatenate([np.cos(angles)] * 2, 1), (1, H))
    low = np.tile(np.concatenate([-np.sin(angles), zeros], 1), (1, H))
    high = np.tile(np.concatenate([zeros, np.sin(angles)], 1), (1, H))
    rows = [
        np.concatenate([np.repeat(t[0::2], 8, 0), np.repeat(t[1::2], 8, 0), np.repeat(t, 4, 0)], 0)
        for t in (cos, low, high)
    ]
    return np.stack(rows).astype(np.float32)


def norm(x, offset, stretch):
    centered = x - jnp.mean(x, axis=-1, keepdims=True)
    variance = jnp.mean(centered * centered, axis=-1, keepdims=True)
    return centered * lax.rsqrt(variance + 1e-06) * (1.0 + stretch) + offset


def kernel(
    lat_h, mod, tab_h, wsq_h, wso_h, wtq_h, wto_h, out,
    lat, tab, wsq, wso, wtq, wto, load_sem,
    nrm, proj, recv, ks, vs, qs, sc, ob, ot, orecv, oa,
    ts, tr, mid, tin, tp, acc, to, toh, ro, roh, bias,
    s_send, s_recv, r_send, r_recv, t_send, t_recv,
    u_send, u_recv, uh_send, uh_recv,
):
    fi, hi = lax.axis_index("frame"), lax.axis_index("head")

    def at_head(k):
        return lax.rem(hi + k, NH)

    def at_frame(k):
        return lax.rem(fi + k, NF)

    def load(src, dst, i):
        return pltpu.make_async_copy(src, dst, load_sem.at[i])

    part_loads = [
        load(wsq_h.at[:, pl.ds(p * D, D)], wsq.at[:, pl.ds(p * D, D)], 2 + p) for p in range(3)
    ]
    loads = [
        load(lat_h, lat, 0), load(tab_h, tab, 1), *part_loads,
        load(wso_h, wso, 5), load(wtq_h, wtq, 6), load(wto_h, wto, 7),
    ]
    for i in (0, 3, 4, 2):
        loads[i].start()

    barrier = pltpu.get_barrier_semaphore()

    def greet(k, _):
        pl.semaphore_signal(barrier, inc=1, device_id=(fi, at_head(k)), device_id_type=MESH)
        return 0

    def greet_frame(k, _):
        pl.semaphore_signal(barrier, inc=1, device_id=(at_frame(k), hi), device_id_type=MESH)
        return 0

    lax.fori_loop(1, NH, greet, 0)
    lax.fori_loop(1, NF, greet_frame, 0)

    def remote(src, dst, send, receive, device):
        return pltpu.make_async_remote_copy(
            src_ref=src, dst_ref=dst, send_sem=send, recv_sem=receive,
            device_id=device, device_id_type=MESH,
        )

    def await_bytes(ref, sem):
        pltpu.make_async_copy(ref, ref, sem).wait()

    loads[0].wait()
    for row, f, p, n in ((0, 0, 0, 192), (192, 1, 128, 64), (256, 1, 0, 128)):
        x = lat[f, p : p + n].astype(F32)
        nrm[row : row + n] = norm(x, mod[0:1], mod[1:2]).astype(BF)

    def piece(phase, ref, part, block):
        rows = (pl.ds(0, 80), pl.ds(80, 64))[phase % 2]
        lanes = (pl.ds(0, 256), pl.ds(256, 128))[phase // 2]
        return ref.at[part, block, rows, lanes]

    def spatial_send(phase, part):
        pltpu.make_async_copy(
            piece(phase, proj, part, hi), piece(phase, recv, part, hi), s_recv.at[phase, part, hi]
        ).start()

        def send(k, _):
            peer = at_head(k)
            remote(
                piece(phase, proj, part, peer), piece(phase, recv, part, hi),
                s_send.at[phase, part, peer], s_recv.at[phase, part, hi], (fi, peer),
            ).start()
            return 0

        lax.fori_loop(1, NH, send, 0)

    for slot, part in enumerate((1, 2, 0)):
        part_loads[part].wait()
        r = dot(nrm[...], wsq[:, part * D : (part + 1) * D])
        proj[slot] = r.astype(BF).T.reshape(NH, PAIR, TOK)
        if slot == 0:
            pl.semaphore_wait(barrier, NH + NF - 2)
        spatial_send(0, slot)
    for phase in range(1, 4):
        for slot in range(3):
            spatial_send(phase, slot)
    for i in (5, 6, 1, 7):
        loads[i].start()

    row = lax.broadcasted_iota(jnp.int32, (256, 256), 0)
    col = lax.broadcasted_iota(jnp.int32, (256, 256), 1)
    bias[0] = jnp.where(row % 8 == col % 8, 0.0, -jnp.inf).astype(F32)
    bias[1] = jnp.where(row % 4 == col % 4, 0.0, -jnp.inf).astype(F32)

    for rows in (slice(0, 16), slice(16 + PAIR, 32 + PAIR)):
        vs[:, rows, :] = jnp.ones((2, 16, KEYS), BF)

    def halves(a, b):
        a, b = a.astype(F32), b.astype(F32)
        lane = lax.broadcasted_iota(jnp.int32, a.shape, 1)
        first = jnp.where(lane < 64, a, pltpu.roll(b, 64, 1))
        second = jnp.where(lane < 64, pltpu.roll(a, 64, 1), b)
        return first.astype(BF), second.astype(BF)

    def prepare(f, h):
        phase = 2 * f + h
        lo, n = ((0, 80), (80, 64))[h]
        own = lax.broadcasted_iota(jnp.int32, (128, 80), 1)
        own = (own < HD) if h == 0 else (own >= 80 - HD)

        def body(j, _):
            sources = (2 * j, 2 * j + 1)
            for src in sources:
                for part in range(3):
                    await_bytes(piece(phase, recv, part, src), s_recv.at[phase, part, src])
            for part, ref, up in ((0, ks, 0), (1, vs, 16)):
                for src in sources:
                    at = pl.multiple_of(src * 128, 128)
                    lanes = slice(0, 128) if f == 0 else slice(256, 384)
                    ref[f, lo + up : lo + up + n, pl.ds(at, 128)] = recv[part, src, lo : lo + n, lanes]
                if f == 0:
                    at = pl.multiple_of(1024 + j * 128, 128)
                    tiles = halves(*(recv[part, src, lo : lo + n, 128:256] for src in sources))
                    for g in range(2):
                        ref[g, lo + up : lo + up + n, pl.ds(at, 128)] = tiles[g]
            for i, src in enumerate(sources):
                rows = slice(64 * h, 64 * h + 80)
                lanes = slice(0, 128) if f == 0 else slice(256, 384)
                q = recv[2, src, rows, lanes].T
                qs[j, i * 128 : i * 128 + 128] = jnp.where(own, q, jnp.zeros_like(q))
                q = recv[2, src, rows, 128:256].T[f * 64 : f * 64 + 64]
                q = jnp.where(own[0:64], q, jnp.zeros_like(q))
                qs[4 + j // 2, pl.ds(pl.multiple_of(j % 2 * 128 + i * 64, 64), 64)] = q
            return 0

        lax.fori_loop(0, NH // 2, body, 0)

    def scores(b, f, h):
        return dot(qs[b], ks[f, 64 * h : 64 * h + 80])

    def mixed(s, f, h):
        p = jnp.exp2((s - jnp.max(s, axis=1, keepdims=True)) * SCALE).astype(BF)
        o = dot(p, vs[f, 80 * h : 80 * h + 96], NT)
        one = 80 * h
        return (o * (1.0 / o[:, one : one + 1])).astype(BF)

    def back_piece(kind, ref, block):
        rows = (pl.ds(0, 64), pl.ds(64, 80))[kind % 2]
        return ref.at[block, rows, pl.ds(kind // 2 * 128, 128)]

    def give(kind, src):
        here, there = back_piece(kind, ot, src), back_piece(kind, orecv, hi)

        @pl.when(src == hi)
        def _():
            pltpu.make_async_copy(here, there, r_recv.at[kind, hi]).start()

        @pl.when(src != hi)
        def _():
            remote(here, there, r_send.at[kind, src], r_recv.at[kind, hi], (fi, src)).start()

    def put(src, h, lanes, o):
        if h == 0:
            ot[src, 0:80, lanes] = o[16:96]
        else:
            row = lax.broadcasted_iota(jnp.int32, (16, o.shape[1]), 0)
            ot[src, 64:80, lanes] = jnp.where(row < 8, ot[src, 64:80, lanes], o[0:16])
            ot[src, 80:PAIR, lanes] = o[16:80]

    def attend(f, h):
        prepare(f, h)
        sc[0] = scores(0, f, h)

        def body(j, _):
            for u in range(2):
                s = sc[u]
                sc[1 - u] = scores(jnp.minimum(2 * j + u + 1, 5), f, h)
                ob[u] = mixed(s, f, h)

            @pl.when(j < 2)
            def _():
                for u in range(2):
                    o = ob[u].T
                    for i in range(2):
                        src = 2 * (2 * j + u) + i
                        lanes = slice(0, 128) if f == 0 else slice(256, 384)
                        put(src, h, lanes, o[:, i * 128 : i * 128 + 128])
                        give(4 * f + h, src)

            @pl.when(j == 2)
            def _():
                for u in range(2):
                    for i in range(4):
                        src = 4 * u + i
                        o = ob[u, i * 64 : i * 64 + 64].T
                        put(src, h, slice(128 + 64 * f, 192 + 64 * f), o)
                        if f == 1:
                            give(2 + h, src)

            return 0

        lax.fori_loop(0, 3, body, 0)

    sub = lax.broadcasted_iota(jnp.int32, (8, D), 0)

    def swap(a, b):
        first = jnp.where(sub < 4, a, pltpu.roll(b, 4, 0))
        second = jnp.where(sub < 4, pltpu.roll(a, 4, 0), b)
        return first, second

    def pack(x):
        return jnp.concatenate([x[:, 0:WIN], x[:, D - WIN : D]], 0).astype(BF)

    def unpack(x):
        x = x.astype(F32)
        return jnp.concatenate([x[0:8], x[8:16, 2 * WIN - D : WIN]], 1)

    def finish_spatial(kind):
        tile = (0, 2, 1)[kind]

        def arrive(src, _):
            for h in range(2):
                await_bytes(back_piece(2 * tile + h, orecv, src), r_recv.at[2 * tile + h, src])
            return 0

        lax.fori_loop(0, NH, arrive, 0)
        rows = slice(kind * 128, kind * 128 + 128)
        oa[rows] = orecv[:, :, tile * 128 : tile * 128 + 128].reshape(D, 128).T
        r = mod[2:3] * dot(oa[rows], wso[...])
        if kind < 2:
            r = lat[kind, 0:128].astype(F32) + r
            for g in range(NF):
                ts[kind, g] = pack(r[g * 8 : g * 8 + 8])
        else:
            x = [lat[f, 128:PATCH].astype(F32) + r[f * 64 : f * 64 + 64] for f in range(2)]
            for g in range(NF // 2):
                a, b = swap(*(y[g * 8 : g * 8 + 8] for y in x))
                ts[2, 2 * g], ts[2, 2 * g + 1] = pack(a), pack(b)

    def exchange(source, target, send, receive):
        pltpu.make_async_copy(source.at[fi], target.at[fi], receive.at[fi]).start()

        def one(k, _):
            peer = at_frame(k)
            remote(
                source.at[peer], target.at[fi], send.at[peer], receive.at[fi], (peer, hi)
            ).start()
            return 0

        lax.fori_loop(1, NF, one, 0)

    def arrived(target, receive):
        def one(k, _):
            src = at_frame(k)
            await_bytes(target.at[src], receive.at[src])
            return 0

        lax.fori_loop(0, NF, one, 0)

    def temporal_project(start, count):
        rows = slice(start, start + count)
        tin[rows] = norm(mid[rows], mod[3:4], mod[4:5]).astype(BF)
        for part in range(3):
            r = dot(tin[rows], wtq[:, part * D : (part + 1) * D]).astype(BF)
            if part < 2:
                r = r.astype(F32)
                low = pltpu.roll(r, D - HD // 2, 1)
                high = pltpu.roll(r, HD // 2, 1)
                r = (r * tab[0, rows] + low * tab[1, rows] + high * tab[2, rows]).astype(BF)
            tp[rows, part * D : (part + 1) * D] = r

    def temporal_head(start, count, offset):
        rows = slice(start, start + count)
        tile = min(offset // 128, 7)
        begin = offset - tile * 128
        lane = lax.broadcasted_iota(jnp.int32, (count, 256), 1)
        own = (lane >= begin) & (lane < begin + HD)

        def part(i):
            return tp[rows, pl.ds(i * D + tile * 128, 256)]

        q = part(0)
        s = dot(jnp.where(own, q, jnp.zeros_like(q)), part(1), NT)
        s = s + bias[0 if count == 256 else 1, 0:count, 0:count]
        e = jnp.exp2((s - jnp.max(s, axis=1, keepdims=True)) * SCALE)
        o = dot(e.astype(BF), part(2)) * (1.0 / jnp.sum(e, axis=1, keepdims=True))
        return own, o, pl.ds(tile * 128, 256)

    def temporal_attend(start, count):
        group = 4
        rows = slice(start, start + count)

        for j in range(H // group):
            done = [temporal_head(start, count, (group * j + b) * HD) for b in range(group)]
            for own, o, lanes in done:
                acc[rows, lanes] = jnp.where(own, o, acc[rows, lanes])
        return mid[rows] + mod[5:6] * dot(acc[rows].astype(BF), wto[...])

    def give_piece(kind):
        finish_spatial(kind)
        exchange(ts.at[kind], tr.at[kind], t_send.at[kind], t_recv.at[kind])

    def take_piece(kind):
        arrived(tr.at[kind], t_recv.at[kind])
        for j in range(NF):
            mid[kind * 128 + j * 8 : kind * 128 + j * 8 + 8] = unpack(tr[kind, j])
        temporal_project(kind * 128, 128)

    attend(0, 0)
    attend(0, 1)
    attend(1, 0)
    for i in (1, 5):
        loads[i].wait()
    give_piece(0)
    attend(1, 1)
    give_piece(1)
    give_piece(2)
    acc[...] = jnp.zeros_like(acc)
    for i in (6, 7):
        loads[i].wait()
    take_piece(0)
    take_piece(1)
    r = temporal_attend(0, 256)
    for j in range(NF):
        both = [r[f * 128 + j * 8 : f * 128 + j * 8 + 8] for f in range(2)]
        to[j] = jnp.concatenate(both, 0).astype(BF)
    exchange(to, ro, u_send, u_recv)
    take_piece(2)
    r = temporal_attend(256, 128)
    for j in range(NF):
        toh[j] = pack(r[j * 8 : j * 8 + 8])
    exchange(toh, roh, uh_send, uh_recv)

    arrived(ro, u_recv)
    for j in range(NF // 2):
        a, b = ro[2 * j].astype(F32), ro[2 * j + 1].astype(F32)
        for f in range(2):
            rows = jnp.concatenate([a[f * 8 : f * 8 + 8], b[f * 8 : f * 8 + 8]], 0)
            out[f, 16 * j : 16 * j + 16] = rows.astype(BF)
    arrived(roh, uh_recv)
    for j in range(NF // 4):
        a, b = (swap(unpack(roh[4 * j + i]), unpack(roh[4 * j + i + 1])) for i in (0, 2))
        for f in range(2):
            rows = jnp.concatenate([a[f], b[f]], 0)
            out[f, 128 + 16 * j : 144 + 16 * j] = rows.astype(BF)

    def sent_head(k, _):
        peer = at_head(k)
        for phase in range(4):
            for part in range(3):
                await_bytes(piece(phase, proj, part, peer), s_send.at[phase, part, peer])
        for kind in range(6):
            await_bytes(back_piece(kind, ot, peer), r_send.at[kind, peer])
        return 0

    lax.fori_loop(1, NH, sent_head, 0)

    def sent_frame(k, _):
        peer = at_frame(k)
        for kind in range(3):
            await_bytes(ts.at[kind, peer], t_send.at[kind, peer])
        await_bytes(to.at[peer], u_send.at[peer])
        await_bytes(toh.at[peer], uh_send.at[peer])
        return 0

    lax.fori_loop(1, NF, sent_frame, 0)


def local(latents, modulation, spatial_qkv, spatial_out, temporal_qkv, temporal_out):
    anywhere = pl.BlockSpec(memory_space=pl.ANY)
    vmem = pl.BlockSpec(memory_space=pltpu.VMEM)
    dma = pltpu.SemaphoreType.DMA
    return pl.pallas_call(
        kernel,
        out_shape=jax.ShapeDtypeStruct((2, PATCH, D), BF),
        in_specs=[anywhere, vmem] + [anywhere] * 5,
        out_specs=vmem,
        scratch_shapes=[
            pltpu.VMEM((2, PATCH, D), BF),
            pltpu.VMEM((3, TOK, D), F32),
            pltpu.VMEM((D, 3 * D), BF),
            pltpu.VMEM((D, D), BF),
            pltpu.VMEM((D, 3 * D), BF),
            pltpu.VMEM((D, D), BF),
            dma((8,)),
            pltpu.VMEM((TOK, D), BF),
            pltpu.VMEM((3, NH, PAIR, TOK), BF),
            pltpu.VMEM((3, NH, PAIR, TOK), BF),
            pltpu.VMEM((2, PAIR, KEYS), BF),
            pltpu.VMEM((2, PAIR + 32, KEYS), BF),
            pltpu.VMEM((6, 256, 80), BF),
            pltpu.VMEM((2, 256, KEYS), F32),
            pltpu.VMEM((2, 256, 96), BF),
            pltpu.VMEM((NH, PAIR, TOK), BF),
            pltpu.VMEM((NH, PAIR, TOK), BF),
            pltpu.VMEM((TOK, D), BF),
            pltpu.VMEM((3, NF, 16, WIN), BF),
            pltpu.VMEM((3, NF, 16, WIN), BF),
            pltpu.VMEM((TOK, D), F32),
            pltpu.VMEM((TOK, D), BF),
            pltpu.VMEM((TOK, 3 * D), BF),
            pltpu.VMEM((TOK, D), F32),
            pltpu.VMEM((NF, 16, D), BF),
            pltpu.VMEM((NF, 16, WIN), BF),
            pltpu.VMEM((NF, 16, D), BF),
            pltpu.VMEM((NF, 16, WIN), BF),
            pltpu.VMEM((2, 256, 256), F32),
            dma((4, 3, NH)), dma((4, 3, NH)), dma((6, NH)), dma((6, NH)),
            dma((3, NF)), dma((3, NF)), dma((NF,)), dma((NF,)),
            dma((NF,)), dma((NF,)),
        ],
        compiler_params=pltpu.CompilerParams(
            collective_id=0, has_side_effects=True, vmem_limit_bytes=62 * 2**20
        ),
    )(
        latents, modulation, jnp.asarray(rope_table()),
        spatial_qkv, spatial_out, temporal_qkv, temporal_out,
    )


def solution(mesh):
    return jax.shard_map(
        local,
        mesh=mesh,
        in_specs=(P("frame", "head", None), P(), P(), P(), P(), P()),
        out_specs=P("frame", "head", None),
        check_vma=False,
    )
```
